32 devices in a mesh: groups: 2 (over y), seq: 4 (over z), pair: 2 (over x), sub: 2 (over core).
Axes of the slice: x: 2, y: 2, z: 4, core: 2. Of those that a mesh axis runs over, the one named last changes fastest.
Arguments:
- embeddings: bfloat16 [64, 256, 1024], P(('groups', 'seq'), 'sub'), parts along dimension 0, may hold values from -8 to 8
- pairs: int32 [128, 2], P(('groups', 'seq', 'pair')), parts along dimension 0, may hold values from 0 to 31, as said below
- lengths: int32 [64], P('groups'), parts along dimension 0, may hold values from 64 to 256
Outputs:
- profile: bfloat16 [64, 256, 1024], P(('groups', 'seq'), 'sub', 'pair'), parts along dimension 0
The draws below stay inside these ranges and needn't reach their ends.
There are 2 independent parts, one for each index of `groups`. The reference program is written for one: setup_inputs(seed, part) draws one part's arguments, and reference() takes and returns one part's arrays. A program takes and returns all parts, laid end to end along the dimension named above; each array names one. Nothing has to cross between parts.
Inputs may be any that keep to these rules, and one draw needn't show every extreme that they name: The rows of pairs form 4 * 2 aligned blocks of 8 rows (the rows of one device); in block k every query id (column 0) lies in (k // 2) * 8 to (k // 2 + 1) * 8 - 1, and for every owner j exactly 2 target ids (column 1) lie in j * 8 to (j + 1) * 8 - 1. A target never equals its query.
All inputs are finite; a program needn't handle non-finite values.
Results may differ from the reference program's by a relative error of at most 0.006.
Values may be sent and summed in bfloat16 or wider, within the bound.
A program may use at most 128 MiB of HBM per device.

```python
import math
import jax
import jax.numpy as jnp
from jax import lax

D = 1024
BL = 256
PROT_DEV = 8
CAP = 2
PAIR_DEV = 8
PROTEINS = 32
PAIRS = 64
N_SEQ = 4
N_PAIR = 2


def draw_embeddings(key, part):
    key = jax.random.fold_in(key, 5)
    key_base, key_scale = jax.random.split(key, 2)
    base = jax.random.normal(key_base, (PROTEINS, BL, D), jnp.float32)
    scale = jnp.exp(jax.random.uniform(key_scale, (PROTEINS, BL, 1), jnp.float32, math.log(0.35), math.log(3.5)))
    values = base * scale
    return jnp.clip(values, -8.0, 8.0).astype(jnp.bfloat16)


def draw_pairs(key, part):
    key = jax.random.fold_in(key, 11)
    key_rest, key_shift = jax.random.split(key, 2)
    block_count = N_SEQ * N_PAIR
    base_owners = (jnp.arange(PAIR_DEV) // CAP).astype(jnp.int32)

    def one_block(block_key):
        key_one, key_three, key_four, key_five = jax.random.split(block_key, 4)
        owners = jax.random.permutation(key_one, base_owners)
        first = jax.random.randint(key_three, (PAIR_DEV,), 0, PROT_DEV)
        second = jax.random.randint(key_four, (PAIR_DEV,), 0, PROT_DEV)
        target_local = jax.random.randint(key_five, (PAIR_DEV,), 0, PROT_DEV)
        return (owners, jnp.minimum(first, second), target_local)
    owners, query_local, target_local = jax.vmap(one_block)(jax.random.split(key_rest, block_count))
    seq_owner = (jnp.arange(block_count) // N_PAIR)[:, None]
    offset = jax.random.randint(key_shift, (block_count, PAIR_DEV), 1, PROT_DEV)
    target_local = jnp.where(owners == seq_owner, (query_local + offset) % PROT_DEV, target_local)
    query_ids = seq_owner * PROT_DEV + query_local
    target_ids = owners * PROT_DEV + target_local
    return jnp.stack([query_ids, target_ids], axis=-1).reshape(PAIRS, 2).astype(jnp.int32)


def set_ends(drawn, key, smallest, top_value):
    longest = drawn.shape.index(max(drawn.shape))
    spots = []
    for shift in (0, 1):
        where = [jax.random.randint(jax.random.fold_in(key, axis), (), 0, length) for axis, length in enumerate(drawn.shape)]
        where[longest] = (where[longest] + shift) % drawn.shape[longest]
        spots.append(tuple(where))
    return drawn.at[spots[0]].set(smallest).at[spots[1]].set(top_value)


def setup_inputs(seed: int = 0, part: int = 0) -> dict:
    key_of = jax.random.split(jax.random.key(seed), 4)
    own_keys = jax.random.split(jax.random.fold_in(key_of[3], part), 4)
    return {
        "embeddings": draw_embeddings(jax.random.fold_in(jax.random.fold_in(key_of[3], part), 71), part),
        "pairs": draw_pairs(jax.random.fold_in(jax.random.fold_in(key_of[3], part), 71), part),
        "lengths": set_ends(jax.random.randint(own_keys[2], (PROTEINS,), BL // 4, BL + 1), jax.random.fold_in(own_keys[2], 1), BL // 4, BL).astype(jnp.int32),
    }


masked_fill = -1e+30

def pair_profile(query_block, target_block, query_length, target_length):
    scores = jnp.dot(query_block, target_block.T, preferred_element_type=jnp.float32) / math.sqrt(D)
    row_valid = jnp.arange(BL)[:, None] < query_length
    col_valid = jnp.arange(BL)[None, :] < target_length
    masked = jnp.where(col_valid, scores, masked_fill)
    row_top = lax.optimization_barrier(jnp.max(masked, axis=1, keepdims=True))
    row_exp = jnp.exp(masked - row_top)
    row_soft = row_exp / lax.optimization_barrier(jnp.sum(row_exp, axis=1, keepdims=True))
    col_masked = jnp.where(row_valid, scores, masked_fill)
    col_top = lax.optimization_barrier(jnp.max(col_masked, axis=0, keepdims=True))
    col_total = lax.optimization_barrier(jnp.sum(jnp.where(row_valid, jnp.exp(col_masked - col_top), 0.0), axis=0, keepdims=True))
    col_soft = jnp.where(row_valid, jnp.exp(scores - col_top), 0.0) / col_total
    weights = jnp.where(row_valid & col_valid, 0.5 * (row_soft + col_soft), 0.0).astype(jnp.bfloat16)
    return jnp.dot(weights, target_block, preferred_element_type=jnp.float32)

def reference(embeddings, pairs, lengths):
    grouped = pairs.reshape(N_SEQ, N_PAIR, PAIR_DEV, 2)
    summed_total = jnp.zeros((PROTEINS, BL, D), jnp.float32)
    for group_index in range(N_PAIR):
        members = grouped[:, group_index].reshape(N_SEQ * PAIR_DEV, 2)

        def add_pair(running, pair_row):
            query_id = pair_row[0].astype(jnp.int32)
            target_id = pair_row[1].astype(jnp.int32)
            aligned = pair_profile(embeddings[query_id], embeddings[target_id], lengths[query_id], lengths[target_id])
            current = lax.dynamic_index_in_dim(running, query_id, 0, keepdims=False)
            running = lax.dynamic_update_index_in_dim(running, current + aligned, query_id, 0)
            return (running, None)
        running, _ = lax.scan(add_pair, jnp.zeros((PROTEINS, BL, D), jnp.float32), members)
        rounded = lax.optimization_barrier(running.astype(jnp.bfloat16))
        summed_total = summed_total + rounded.astype(jnp.float32)
    counts = lax.optimization_barrier(jnp.sum((pairs[:, 0][:, None] == jnp.arange(PROTEINS, dtype=jnp.int32)[None, :]).astype(jnp.int32), axis=0))
    divisor = jnp.maximum(counts, 1).astype(jnp.float32)
    return (summed_total / divisor[:, None, None]).astype(jnp.bfloat16)
```

```python
import functools
import math

import jax
import jax.numpy as jnp
from jax import lax
from jax.experimental import pallas as pl
from jax.experimental.pallas import tpu as pltpu
from jax.sharding import PartitionSpec as P

masked_fill = -1e30
MESH = pl.DeviceIdType.MESH


def kernel(
    seq_count,
    pair_count,
    pairs_ref,
    pairs_vmem,
    lengths_ref,
    emb_ref,
    out_ref,
    info_seq_vmem,
    info_pair_vmem,
    info_seq,
    info_pair,
    query_table,
    target_table,
    other_query_table,
    emb_other,
    outgoing,
    t_own,
    t_other,
    w_own,
    w_other,
    acc,
    seq_info_send,
    seq_info_recv,
    pair_info_send,
    pair_info_recv,
    query_send,
    query_recv,
    smem_sem,
    z_send,
    z_recv,
    s_send,
    s_recv,
    xt_send,
    xt_recv,
    xs_send,
    xs_recv,
    xw_send,
    xw_recv,
):
    me = lax.axis_index("seq")
    mine = lax.axis_index("pair")
    sub = lax.axis_index("sub")
    sibling = 1 - sub
    prot_dev, half, width = emb_ref.shape
    full = 2 * half
    pair_dev = pairs_ref.shape[0]
    capacity = pair_dev // seq_count
    slots = pair_dev
    features = width // pair_count
    own_rows = pl.ds(pl.multiple_of(sub * half, half), half)
    sibling_rows = pl.ds(pl.multiple_of(sibling * half, half), half)
    own_features = pl.ds(pl.multiple_of(mine * features, features), features)

    def seq_peer(distance):
        return {"seq": lax.rem(me + distance, seq_count)}

    def pair_peer(distance):
        return {"pair": lax.rem(mine + distance, pair_count)}

    def remote(src, dst, send, recv, device):
        return pltpu.make_async_remote_copy(
            src_ref=src, dst_ref=dst, send_sem=send, recv_sem=recv, device_id=device,
            device_id_type=MESH,
        )

    def seq_info_copy(d):
        return remote(
            pairs_vmem, info_seq_vmem.at[d - 1], seq_info_send.at[d - 1], seq_info_recv.at[d - 1],
            seq_peer(d),
        )

    def pair_info_copy(d):
        there = pair_count - d - 1
        return remote(
            pairs_vmem, info_pair_vmem.at[there], pair_info_send.at[there],
            pair_info_recv.at[there], pair_peer(d),
        )

    def query_copy():
        return remote(emb_ref, emb_other, query_send, query_recv, {"sub": sibling})

    def z_copy(d, i):
        return remote(
            outgoing.at[i - capacity], t_own.at[i, own_rows, :], z_send.at[i], z_recv.at[i],
            seq_peer(d),
        )

    def s_copy(i, rows):
        return remote(
            t_own.at[i, rows, :], t_own.at[i, rows, :], s_send.at[i], s_recv.at[i],
            {"sub": sibling},
        )

    def xt_copy(d, i):
        there = pair_count - d - 1
        peer = lax.rem(mine + d, pair_count)
        columns = pl.ds(pl.multiple_of(peer * features, features), features)
        return remote(
            t_own.at[i, own_rows, columns], t_other.at[there, i, own_rows, :],
            xt_send.at[there, i], xt_recv.at[there, i], pair_peer(d),
        )

    def xs_copy(e, i, rows):
        return remote(
            t_other.at[e, i, rows, :], t_other.at[e, i, rows, :], xs_send.at[e, i],
            xs_recv.at[e, i], {"sub": sibling},
        )

    def xw_copy(d, i):
        there = pair_count - d - 1
        return remote(
            w_own.at[i], w_other.at[there, i], xw_send.at[there, i], xw_recv.at[there, i],
            pair_peer(d),
        )

    barrier = pltpu.get_barrier_semaphore()
    for d in range(1, seq_count):
        pl.semaphore_signal(barrier, inc=1, device_id=seq_peer(d), device_id_type=MESH)
    for d in range(1, pair_count):
        pl.semaphore_signal(barrier, inc=1, device_id=pair_peer(d), device_id_type=MESH)
    pl.semaphore_signal(barrier, inc=1, device_id={"sub": sibling}, device_id_type=MESH)
    pl.semaphore_wait(barrier, seq_count + pair_count - 1)

    for d in range(1, seq_count):
        seq_info_copy(d).start()
    for d in range(1, pair_count):
        pair_info_copy(d).start()
    query_copy().start()

    def find(table, owner, rank):
        def look(n, state):
            seen, query, target = state
            query_id = table[n, 0]
            target_id = table[n, 1]
            match = lax.div(target_id, prot_dev) == owner
            take = jnp.logical_and(match, seen == rank)
            query = jnp.where(take, query_id, query)
            target = jnp.where(take, target_id, target)
            seen = seen + jnp.where(match, 1, 0)
            return (seen, query, target)

        zero = jnp.int32(0)
        _, query, target = lax.fori_loop(0, pair_dev, look, (zero, zero, zero))
        return query, target

    for d in range(1, seq_count):
        seq_info_copy(d).wait_recv()
    for d in range(1, pair_count):
        pair_info_copy(d).wait_recv()
    local_seq = pltpu.make_async_copy(info_seq_vmem, info_seq, smem_sem.at[0])
    local_pair = pltpu.make_async_copy(info_pair_vmem, info_pair, smem_sem.at[1])
    local_seq.start()
    local_pair.start()
    local_seq.wait()
    local_pair.wait()

    def send_targets(step, carry):
        d = lax.div(step, capacity) + 1
        rank = lax.rem(step, capacity)
        asker = info_seq.at[seq_count - d - 1]
        _, target = find(asker, me, rank)
        outgoing[step] = emb_ref[lax.rem(target, prot_dev)]
        z_copy(d, step + capacity).start()
        return carry

    lax.fori_loop(0, slots - capacity, send_targets, 0)

    def fill_tables(i, carry):
        d = lax.div(i, capacity)
        rank = lax.rem(i, capacity)
        owner = lax.rem(me - d + seq_count, seq_count)
        query, target = find(pairs_ref, owner, rank)
        query_table[i] = lax.rem(query, prot_dev)
        target_table[i] = target

        def others(e, inner):
            other_query, _ = find(info_pair.at[e], owner, rank)
            other_query_table[e, i] = lax.rem(other_query, prot_dev)
            return inner

        return lax.fori_loop(0, pair_count - 1, others, carry)

    lax.fori_loop(0, slots, fill_tables, 0)

    def own_targets(i, carry):
        t_own[i, own_rows, :] = emb_ref[lax.rem(target_table[i], prot_dev)]
        return carry

    lax.fori_loop(0, capacity, own_targets, 0)
    acc[...] = jnp.zeros_like(acc)
    query_copy().wait_recv()

    scale = 1.0 / math.sqrt(width)
    contract = (((1,), (1,)), ((), ()))

    def weights(i):
        query = query_table[i]
        target = target_table[i]
        query_length = lengths_ref[query + me * prot_dev]
        target_length = lengths_ref[target]
        block = t_own[i]
        own = scale * lax.dot_general(
            emb_ref[query], block, contract, preferred_element_type=jnp.float32
        )
        other = scale * lax.dot_general(
            emb_other[query], block, contract, preferred_element_type=jnp.float32
        )
        rows = lax.broadcasted_iota(jnp.int32, (half, full), 0)
        columns = lax.broadcasted_iota(jnp.int32, (half, full), 1)
        own_live = rows + sub * half < query_length
        other_live = rows + sibling * half < query_length
        col_live = columns < target_length
        col_top = jnp.maximum(
            jnp.max(jnp.where(own_live, own, masked_fill), axis=0, keepdims=True),
            jnp.max(jnp.where(other_live, other, masked_fill), axis=0, keepdims=True),
        )
        own_exp = jnp.where(own_live, jnp.exp(own - col_top), 0.0)
        other_exp = jnp.where(other_live, jnp.exp(other - col_top), 0.0)
        col_total = jnp.sum(own_exp, axis=0, keepdims=True) + jnp.sum(
            other_exp, axis=0, keepdims=True
        )
        masked = jnp.where(col_live, own, masked_fill)
        row_exp = jnp.exp(masked - jnp.max(masked, axis=1, keepdims=True))
        row_total = jnp.sum(row_exp, axis=1, keepdims=True)
        both = row_exp * (0.5 / row_total) + own_exp * (0.5 / col_total)
        w_own[i] = jnp.where(jnp.logical_and(own_live, col_live), both, 0.0).astype(jnp.bfloat16)

    def add(weight, block, query):
        result = jnp.dot(weight, block, preferred_element_type=jnp.float32)
        for a in range(prot_dev):
            acc[a] += jnp.where(query == a, result, 0.0)

    def step(i, carry):
        @pl.when(i < slots)
        def _():
            @pl.when(i >= capacity)
            def _():
                z_copy(1, i).wait_recv()

            s_copy(i, own_rows).start()
            for d in range(1, pair_count):
                xt_copy(d, i).start()

        @pl.when(jnp.logical_and(i >= 1, i <= slots))
        def _():
            k = i - 1
            for e in range(pair_count - 1):
                xt_copy(pair_count - 1 - e, k).wait_recv()
                xs_copy(e, k, own_rows).start()
            s_copy(k, sibling_rows).wait_recv()
            weights(k)
            for d in range(1, pair_count):
                xw_copy(d, k).start()
            add(w_own[k], t_own[k, :, own_features], query_table[k])

        @pl.when(i >= 2)
        def _():
            k = i - 2

            def remote_add(e, inner):
                xw_copy(pair_count - 1 - e, k).wait_recv()
                xs_copy(e, k, sibling_rows).wait_recv()
                add(w_other[e, k], t_other[e, k], other_query_table[e, k])
                return inner

            lax.fori_loop(0, pair_count - 1, remote_add, 0)

        return carry

    lax.fori_loop(0, slots + 2, step, 0)

    def count_of(table, start):
        def look(n, counts):
            query = lax.rem(table[n, 0], prot_dev)
            return tuple(c + jnp.where(query == a, 1, 0) for a, c in enumerate(counts))

        return lax.fori_loop(0, pair_dev, look, start)

    counts = count_of(pairs_ref, (jnp.int32(0),) * prot_dev)
    counts = lax.fori_loop(
        0, pair_count - 1, lambda e, state: count_of(info_pair.at[e], state), counts
    )
    for a in range(prot_dev):
        divisor = jnp.maximum(counts[a], 1).astype(jnp.float32)
        out_ref[a] = (acc[a] / divisor).astype(out_ref.dtype)

    for d in range(1, seq_count):
        seq_info_copy(d).wait_send()
    for d in range(1, pair_count):
        pair_info_copy(d).wait_send()
    query_copy().wait_send()

    def finish(i, carry):
        @pl.when(i >= capacity)
        def _():
            z_copy(1, i).wait_send()

        s_copy(i, own_rows).wait_send()
        for d in range(1, pair_count):
            xt_copy(d, i).wait_send()
            xs_copy(d - 1, i, own_rows).wait_send()
            xw_copy(d, i).wait_send()
        return carry

    lax.fori_loop(0, slots, finish, 0)


def local(seq_count, pair_count, embeddings, pairs, lengths):
    prot_dev, half, width = embeddings.shape
    pair_dev = pairs.shape[0]
    full = 2 * half
    features = width // pair_count
    capacity = pair_dev // seq_count
    others = pair_count - 1
    smem = pl.BlockSpec(memory_space=pltpu.SMEM)
    vmem = pl.BlockSpec(memory_space=pltpu.VMEM)
    dma = pltpu.SemaphoreType.DMA
    bf16 = jnp.bfloat16
    return pl.pallas_call(
        functools.partial(kernel, seq_count, pair_count),
        out_shape=jax.ShapeDtypeStruct((prot_dev, half, features), bf16),
        in_specs=[smem, vmem, smem, vmem],
        out_specs=vmem,
        scratch_shapes=[
            pltpu.VMEM((seq_count - 1, pair_dev, 2), jnp.int32),
            pltpu.VMEM((others, pair_dev, 2), jnp.int32),
            pltpu.SMEM((seq_count - 1, pair_dev, 2), jnp.int32),
            pltpu.SMEM((others, pair_dev, 2), jnp.int32),
            pltpu.SMEM((pair_dev,), jnp.int32),
            pltpu.SMEM((pair_dev,), jnp.int32),
            pltpu.SMEM((others, pair_dev), jnp.int32),
            pltpu.VMEM((prot_dev, half, width), bf16),
            pltpu.VMEM((pair_dev - capacity, half, width), bf16),
            pltpu.VMEM((pair_dev, full, width), bf16),
            pltpu.VMEM((others, pair_dev, full, features), bf16),
            pltpu.VMEM((pair_dev, half, full), bf16),
            pltpu.VMEM((others, pair_dev, half, full), bf16),
            pltpu.VMEM((prot_dev, half, features), jnp.float32),
            dma((seq_count - 1,)),
            dma((seq_count - 1,)),
            dma((others,)),
            dma((others,)),
            dma,
            dma,
            dma((2,)),
            dma((pair_dev,)),
            dma((pair_dev,)),
            dma((pair_dev,)),
            dma((pair_dev,)),
            dma((others, pair_dev)),
            dma((others, pair_dev)),
            dma((others, pair_dev)),
            dma((others, pair_dev)),
            dma((others, pair_dev)),
            dma((others, pair_dev)),
        ],
        compiler_params=pltpu.CompilerParams(
            collective_id=0, has_side_effects=True, vmem_limit_bytes=60 * 1024 * 1024
        ),
    )(pairs, pairs, lengths, embeddings)


def solution(mesh):
    placed = (P(("groups", "seq"), "sub", None), P(("groups", "seq", "pair"), None), P("groups"))
    return jax.shard_map(
        functools.partial(local, mesh.shape["seq"], mesh.shape["pair"]),
        mesh=mesh,
        in_specs=placed,
        out_specs=P(("groups", "seq"), "sub", "pair"),
        check_vma=False,
    )
```

```python
import functools
import math

import jax
import jax.numpy as jnp
from jax import lax
from jax.experimental import pallas as pl
from jax.experimental.pallas import tpu as pltpu
from jax.sharding import PartitionSpec as P

masked_fill = -1e30
window = 2
lag = 1
shift = 0
MESH = pl.DeviceIdType.MESH


def kernel(
    seq_count,
    pair_count,
    pairs_ref,
    lengths_ref,
    emb_hbm,
    out_ref,
    table,
    seq_tables,
    pair_tables,
    emb_ref,
    emb_other,
    outgoing,
    t_own,
    r_out,
    r_in,
    acc,
    load_sem,
    seq_info_send,
    seq_info_recv,
    pair_info_send,
    pair_info_recv,
    query_send,
    query_recv,
    z_send,
    z_recv,
    s_send,
    s_recv,
    x_send,
    x_recv,
):
    me = lax.axis_index("seq")
    mine = lax.axis_index("pair")
    sub = lax.axis_index("sub")
    sibling = 1 - sub
    prot_dev, half, width = emb_ref.shape
    full = 2 * half
    pair_dev = pairs_ref.shape[1]
    capacity = pair_dev // seq_count
    slots = pair_dev
    features = width // pair_count
    own_rows = pl.ds(pl.multiple_of(sub * half, half), half)
    sibling_rows = pl.ds(pl.multiple_of(sibling * half, half), half)

    def slot_key(i):
        j = i - capacity
        later = i >= capacity
        d = jnp.where(later, lax.rem(j + shift, seq_count - 1) + 1, 0)
        rank = jnp.where(later, lax.div(j, seq_count - 1), i)
        return d, rank

    def partner(d):
        result = jnp.int32(0)
        bit = 1
        while bit < seq_count:
            result += lax.rem(lax.div(me, bit) + lax.div(jnp.int32(d), bit), 2) * bit
            bit *= 2
        return result

    def seq_peer(d):
        return {"seq": partner(d)}

    def pair_peer(distance):
        return {"pair": lax.rem(mine + distance, pair_count)}

    def feature_block(index):
        return pl.ds(pl.multiple_of(index * features, features), features)

    def remote(src, dst, send, recv, device):
        return pltpu.make_async_remote_copy(
            src_ref=src, dst_ref=dst, send_sem=send, recv_sem=recv, device_id=device,
            device_id_type=MESH,
        )

    def seq_info_copy(d):
        return remote(
            table, seq_tables.at[d - 1], seq_info_send.at[d - 1], seq_info_recv.at[d - 1],
            seq_peer(d),
        )

    def pair_info_copy(d):
        there = pair_count - d - 1
        return remote(
            table, pair_tables.at[there], pair_info_send.at[there], pair_info_recv.at[there],
            pair_peer(d),
        )

    def query_copy():
        return remote(emb_ref, emb_other, query_send, query_recv, {"sub": sibling})

    def z_copy(d, i):
        return remote(
            outgoing.at[i - capacity], t_own.at[i, own_rows, :], z_send.at[i - capacity],
            z_recv.at[i - capacity], seq_peer(d),
        )

    def s_copy(i, rows):
        return remote(
            t_own.at[i, rows, :], t_own.at[i, rows, :], s_send.at[i - capacity],
            s_recv.at[i - capacity], {"sub": sibling},
        )

    def x_copy(d, i):
        there = pair_count - d - 1
        return remote(
            r_out.at[there, i], r_in.at[there, i], x_send.at[there, i], x_recv.at[there, i],
            pair_peer(d),
        )

    load = pltpu.make_async_copy(emb_hbm, emb_ref, load_sem)
    load.start()
    barrier = pltpu.get_barrier_semaphore()
    for d in range(1, seq_count):
        pl.semaphore_signal(barrier, inc=1, device_id=seq_peer(d), device_id_type=MESH)
    for d in range(1, pair_count):
        pl.semaphore_signal(barrier, inc=1, device_id=pair_peer(d), device_id_type=MESH)
    pl.semaphore_signal(barrier, inc=1, device_id={"sub": sibling}, device_id_type=MESH)

    def fill_table(i, carry):
        d, rank = slot_key(i)
        owner = partner(d)

        def look(n, state):
            seen, query, target = state
            query_id = pairs_ref[0, n]
            target_id = pairs_ref[1, n]
            match = lax.div(target_id, prot_dev) == owner
            take = jnp.logical_and(match, seen == rank)
            query = jnp.where(take, query_id, query)
            target = jnp.where(take, target_id, target)
            seen = seen + jnp.where(match, 1, 0)
            return (seen, query, target)

        zero = jnp.int32(0)
        _, query, target = lax.fori_loop(
            0, pair_dev, look, (zero, zero, zero), unroll=pair_dev <= 8
        )
        table[0, i] = query
        table[1, i] = target
        return carry

    lax.fori_loop(0, slots, fill_table, 0)
    pl.semaphore_wait(barrier, seq_count + pair_count - 1)

    for d in range(1, seq_count):
        seq_info_copy(d).start()
    for d in range(1, pair_count):
        pair_info_copy(d).start()
    load.wait()
    for d in range(1, seq_count):
        seq_info_copy(d).wait_recv()

    def send_targets(i, carry):
        d, _ = slot_key(i)
        outgoing[i - capacity] = emb_ref[lax.rem(seq_tables[d - 1, 1, i], prot_dev)]

        @pl.when(i < capacity + window)
        def _():
            z_copy(d, i).start()

        return carry

    lax.fori_loop(capacity, slots, send_targets, 0)
    query_copy().start()
    for d in range(1, pair_count):
        pair_info_copy(d).wait_recv()

    def own_targets(i, carry):
        t_own[i, own_rows, :] = emb_ref[lax.rem(table[1, i], prot_dev)]
        return carry

    lax.fori_loop(0, capacity, own_targets, 0)
    acc[...] = jnp.zeros_like(acc)
    query_copy().wait_recv()

    def sibling_targets(i, carry):
        t_own[i, sibling_rows, :] = emb_other[lax.rem(table[1, i], prot_dev)]
        return carry

    lax.fori_loop(0, capacity, sibling_targets, 0)

    scale = 1.0 / math.sqrt(width)
    contract = (((1,), (1,)), ((), ()))

    def weights(i):
        query_id = table[0, i]
        query = lax.rem(query_id, prot_dev)
        query_length = lengths_ref[query_id]
        target_length = lengths_ref[table[1, i]]
        block = t_own[i]
        own = scale * lax.dot_general(
            emb_ref[query], block, contract, preferred_element_type=jnp.float32
        )
        other = scale * lax.dot_general(
            emb_other[query], block, contract, preferred_element_type=jnp.float32
        )
        rows = lax.broadcasted_iota(jnp.int32, (half, full), 0)
        columns = lax.broadcasted_iota(jnp.int32, (half, full), 1)
        own_live = rows + sub * half < query_length
        other_live = rows + sibling * half < query_length
        col_live = columns < target_length
        col_top = jnp.maximum(
            jnp.max(jnp.where(own_live, own, masked_fill), axis=0, keepdims=True),
            jnp.max(jnp.where(other_live, other, masked_fill), axis=0, keepdims=True),
        )
        own_exp = jnp.where(own_live, jnp.exp(own - col_top), 0.0)
        other_exp = jnp.where(other_live, jnp.exp(other - col_top), 0.0)
        col_total = jnp.sum(own_exp, axis=0, keepdims=True) + jnp.sum(
            other_exp, axis=0, keepdims=True
        )
        masked = jnp.where(col_live, own, masked_fill)
        row_exp = jnp.exp(masked - jnp.max(masked, axis=1, keepdims=True))
        row_total = jnp.sum(row_exp, axis=1, keepdims=True)
        both = row_exp * (0.5 / row_total) + own_exp * (0.5 / col_total)
        return jnp.where(jnp.logical_and(own_live, col_live), both, 0.0).astype(jnp.bfloat16)

    def aligned(weight, i, index):
        return jnp.dot(
            weight, t_own[i, :, feature_block(index)], preferred_element_type=jnp.float32
        )

    def add(result, query_id):
        query = lax.rem(query_id, prot_dev)
        for a in range(prot_dev):
            acc[a] += jnp.where(query == a, result, 0.0)

    def step(i, carry):
        @pl.when(jnp.logical_and(i >= capacity, i < slots))
        def _():
            z_copy(1, i).wait_recv()

            @pl.when(i + window < slots)
            def _():
                z_copy(slot_key(i + window)[0], i + window).start()

            s_copy(i, own_rows).start()

        def tail(k):
            def remote_add(e, inner):
                x_copy(pair_count - 1 - e, k).wait_recv()
                add(r_in[e, k].astype(jnp.float32), pair_tables[e, 0, k])
                return inner

            lax.fori_loop(0, pair_count - 1, remote_add, 0)

        @pl.when(jnp.logical_and(i >= lag, i < slots + lag))
        def _():
            k = i - lag

            @pl.when(k >= capacity)
            def _():
                s_copy(k, sibling_rows).wait_recv()

            weight = weights(k)
            for d in range(1, pair_count):
                there = pair_count - d - 1
                peer = lax.rem(mine + d, pair_count)
                r_out[there, k] = aligned(weight, k, peer).astype(jnp.bfloat16)
                x_copy(d, k).start()
            add(aligned(weight, k, mine), table[0, k])

        @pl.when(i >= lag + 1)
        def _():
            tail(i - lag - 1)

        return carry

    lax.fori_loop(0, slots + lag + 1, step, 0)

    def count(n, counts, ids):
        query = lax.rem(ids(n), prot_dev)
        return tuple(c + jnp.where(query == a, 1, 0) for a, c in enumerate(counts))

    counts = lax.fori_loop(
        0,
        slots,
        lambda n, state: count(n, state, lambda m: table[0, m]),
        (jnp.int32(0),) * prot_dev,
    )
    for e in range(pair_count - 1):
        counts = lax.fori_loop(
            0, slots, lambda n, state: count(n, state, lambda m: pair_tables[e, 0, m]), counts
        )
    for a in range(prot_dev):
        divisor = jnp.maximum(counts[a], 1).astype(jnp.float32)
        out_ref[a] = (acc[a] / divisor).astype(out_ref.dtype)

    for d in range(1, seq_count):
        seq_info_copy(d).wait_send()
    for d in range(1, pair_count):
        pair_info_copy(d).wait_send()
    query_copy().wait_send()

    def finish(i, carry):
        @pl.when(i >= capacity)
        def _():
            z_copy(1, i).wait_send()
            s_copy(i, own_rows).wait_send()

        for d in range(1, pair_count):
            x_copy(d, i).wait_send()
        return carry

    lax.fori_loop(0, slots, finish, 0)


def local(seq_count, pair_count, embeddings, pairs, lengths):
    prot_dev, half, width = embeddings.shape
    pair_dev = pairs.shape[0]
    full = 2 * half
    features = width // pair_count
    capacity = pair_dev // seq_count
    moved = pair_dev - capacity
    others = pair_count - 1
    smem = pl.BlockSpec(memory_space=pltpu.SMEM)
    vmem = pl.BlockSpec(memory_space=pltpu.VMEM)
    dma = pltpu.SemaphoreType.DMA
    bf16 = jnp.bfloat16
    return pl.pallas_call(
        functools.partial(kernel, seq_count, pair_count),
        out_shape=jax.ShapeDtypeStruct((prot_dev, half, features), bf16),
        in_specs=[smem, smem, pl.BlockSpec(memory_space=pl.ANY)],
        out_specs=vmem,
        scratch_shapes=[
            pltpu.SMEM((2, pair_dev), jnp.int32),
            pltpu.SMEM((seq_count - 1, 2, pair_dev), jnp.int32),
            pltpu.SMEM((others, 2, pair_dev), jnp.int32),
            pltpu.VMEM((prot_dev, half, width), bf16),
            pltpu.VMEM((prot_dev, half, width), bf16),
            pltpu.VMEM((moved, half, width), bf16),
            pltpu.VMEM((pair_dev, full, width), bf16),
            pltpu.VMEM((others, pair_dev, half, features), bf16),
            pltpu.VMEM((others, pair_dev, half, features), bf16),
            pltpu.VMEM((prot_dev, half, features), jnp.float32),
            dma,
            dma((seq_count - 1,)),
            dma((seq_count - 1,)),
            dma((others,)),
            dma((others,)),
            dma,
            dma,
            dma((moved,)),
            dma((moved,)),
            dma((moved,)),
            dma((moved,)),
            dma((others, pair_dev)),
            dma((others, pair_dev)),
        ],
        compiler_params=pltpu.CompilerParams(
            collective_id=0, has_side_effects=True, vmem_limit_bytes=60 * 1024 * 1024
        ),
    )(pairs.T, lengths, embeddings)


def solution(mesh):
    placed = (P(("groups", "seq"), "sub", None), P(("groups", "seq", "pair"), None), P("groups"))
    return jax.shard_map(
        functools.partial(local, mesh.shape["seq"], mesh.shape["pair"]),
        mesh=mesh,
        in_specs=placed,
        out_specs=P(("groups", "seq"), "sub", "pair"),
        check_vma=False,
    )
```

```python
import functools
import math

import jax
import jax.numpy as jnp
from jax import lax
from jax.experimental import pallas as pl
from jax.experimental.pallas import tpu as pltpu
from jax.sharding import PartitionSpec as P

masked_fill = -1e30
window = 3
lag = 0
shift = 0
MESH = pl.DeviceIdType.MESH


def kernel(
    seq_count,
    pair_count,
    pairs_ref,
    lengths_ref,
    emb_hbm,
    out_hbm,
    table,
    seq_tables,
    pair_tables,
    emb_ref,
    emb_other,
    outgoing,
    t_own,
    r_out,
    r_in,
    acc,
    out_buf,
    out_sem,
    load_sem,
    seq_info_send,
    seq_info_recv,
    pair_info_send,
    pair_info_recv,
    query_send,
    query_recv,
    z_send,
    z_recv,
    s_send,
    s_recv,
    x_send,
    x_recv,
):
    me = lax.axis_index("seq")
    mine = lax.axis_index("pair")
    sub = lax.axis_index("sub")
    sibling = 1 - sub
    prot_dev, half, width = emb_ref.shape
    full = 2 * half
    pair_dev = pairs_ref.shape[1]
    capacity = pair_dev // seq_count
    slots = pair_dev
    features = width // pair_count
    own_rows = pl.ds(pl.multiple_of(sub * half, half), half)
    sibling_rows = pl.ds(pl.multiple_of(sibling * half, half), half)

    def slot_key(i):
        j = i - capacity
        later = i >= capacity
        d = jnp.where(later, lax.rem(j + shift, seq_count - 1) + 1, 0)
        rank = jnp.where(later, lax.div(j, seq_count - 1), i)
        return d, rank

    def partner(d):
        result = jnp.int32(0)
        bit = 1
        while bit < seq_count:
            result += lax.rem(lax.div(me, bit) + lax.div(jnp.int32(d), bit), 2) * bit
            bit *= 2
        return result

    def seq_peer(d):
        return {"seq": partner(d)}

    def pair_peer(distance):
        return {"pair": lax.rem(mine + distance, pair_count)}

    def feature_block(index):
        return pl.ds(pl.multiple_of(index * features, features), features)

    def remote(src, dst, send, recv, device):
        return pltpu.make_async_remote_copy(
            src_ref=src, dst_ref=dst, send_sem=send, recv_sem=recv, device_id=device,
            device_id_type=MESH,
        )

    def seq_info_copy(d):
        return remote(
            table, seq_tables.at[d - 1], seq_info_send.at[d - 1], seq_info_recv.at[d - 1],
            seq_peer(d),
        )

    def pair_info_copy(d):
        there = pair_count - d - 1
        return remote(
            table, pair_tables.at[there], pair_info_send.at[there], pair_info_recv.at[there],
            pair_peer(d),
        )

    def query_copy():
        return remote(emb_ref, emb_other, query_send, query_recv, {"sub": sibling})

    def z_copy(d, i):
        return remote(
            outgoing.at[i - capacity], t_own.at[i, own_rows, :], z_send.at[i - capacity],
            z_recv.at[i - capacity], seq_peer(d),
        )

    def s_copy(i, rows):
        return remote(
            t_own.at[i, rows, :], t_own.at[i, rows, :], s_send.at[i - capacity],
            s_recv.at[i - capacity], {"sub": sibling},
        )

    def x_copy(d, i):
        there = pair_count - d - 1
        return remote(
            r_out.at[there, i], r_in.at[there, i], x_send.at[there, i], x_recv.at[there, i],
            pair_peer(d),
        )

    def out_copy(a):
        return pltpu.make_async_copy(out_buf.at[a], out_hbm.at[a], out_sem.at[a])

    load = pltpu.make_async_copy(emb_hbm, emb_ref, load_sem)
    load.start()
    barrier = pltpu.get_barrier_semaphore()
    for d in range(1, seq_count):
        pl.semaphore_signal(barrier, inc=1, device_id=seq_peer(d), device_id_type=MESH)
    for d in range(1, pair_count):
        pl.semaphore_signal(barrier, inc=1, device_id=pair_peer(d), device_id_type=MESH)
    pl.semaphore_signal(barrier, inc=1, device_id={"sub": sibling}, device_id_type=MESH)

    def fill_table(i, carry):
        d, rank = slot_key(i)
        owner = partner(d)

        def look(n, state):
            seen, query, target = state
            query_id = pairs_ref[0, n]
            target_id = pairs_ref[1, n]
            match = lax.div(target_id, prot_dev) == owner
            take = jnp.logical_and(match, seen == rank)
            query = jnp.where(take, query_id, query)
            target = jnp.where(take, target_id, target)
            seen = seen + jnp.where(match, 1, 0)
            return (seen, query, target)

        zero = jnp.int32(0)
        _, query, target = lax.fori_loop(
            0, pair_dev, look, (zero, zero, zero), unroll=pair_dev <= 8
        )
        table[0, i] = query
        table[1, i] = target
        return carry

    lax.fori_loop(0, slots, fill_table, 0)
    pl.semaphore_wait(barrier, seq_count + pair_count - 1)

    for d in range(1, seq_count):
        seq_info_copy(d).start()
    for d in range(1, pair_count):
        pair_info_copy(d).start()
    load.wait()
    for d in range(1, seq_count):
        seq_info_copy(d).wait_recv()

    def send_targets(i, carry):
        d, _ = slot_key(i)
        outgoing[i - capacity] = emb_ref[lax.rem(seq_tables[d - 1, 1, i], prot_dev)]

        @pl.when(i < capacity + window)
        def _():
            z_copy(d, i).start()

        return carry

    lax.fori_loop(capacity, slots, send_targets, 0)
    query_copy().start()
    for d in range(1, pair_count):
        pair_info_copy(d).wait_recv()

    def own_targets(i, carry):
        t_own[i, own_rows, :] = emb_ref[lax.rem(table[1, i], prot_dev)]
        return carry

    lax.fori_loop(0, capacity, own_targets, 0)
    acc[...] = jnp.zeros_like(acc)
    query_copy().wait_recv()

    def sibling_targets(i, carry):
        t_own[i, sibling_rows, :] = emb_other[lax.rem(table[1, i], prot_dev)]
        return carry

    lax.fori_loop(0, capacity, sibling_targets, 0)

    scale = 1.0 / math.sqrt(width)
    contract = (((1,), (1,)), ((), ()))

    def weights(i):
        query_id = table[0, i]
        query = lax.rem(query_id, prot_dev)
        query_length = lengths_ref[query_id]
        target_length = lengths_ref[table[1, i]]
        block = t_own[i]
        own = scale * lax.dot_general(
            emb_ref[query], block, contract, preferred_element_type=jnp.float32
        )
        other = scale * lax.dot_general(
            emb_other[query], block, contract, preferred_element_type=jnp.float32
        )
        rows = lax.broadcasted_iota(jnp.int32, (half, full), 0)
        columns = lax.broadcasted_iota(jnp.int32, (half, full), 1)
        own_live = rows + sub * half < query_length
        other_live = rows + sibling * half < query_length
        col_live = columns < target_length
        col_top = jnp.maximum(
            jnp.max(jnp.where(own_live, own, masked_fill), axis=0, keepdims=True),
            jnp.max(jnp.where(other_live, other, masked_fill), axis=0, keepdims=True),
        )
        own_exp = jnp.where(own_live, jnp.exp(own - col_top), 0.0)
        other_exp = jnp.where(other_live, jnp.exp(other - col_top), 0.0)
        col_total = jnp.sum(own_exp, axis=0, keepdims=True) + jnp.sum(
            other_exp, axis=0, keepdims=True
        )
        masked = jnp.where(col_live, own, masked_fill)
        row_exp = jnp.exp(masked - jnp.max(masked, axis=1, keepdims=True))
        row_total = jnp.sum(row_exp, axis=1, keepdims=True)
        both = row_exp * (0.5 / row_total) + own_exp * (0.5 / col_total)
        return jnp.where(jnp.logical_and(own_live, col_live), both, 0.0).astype(jnp.bfloat16)

    def aligned(weight, i, index):
        return jnp.dot(
            weight, t_own[i, :, feature_block(index)], preferred_element_type=jnp.float32
        )

    def add(result, query_id):
        query = lax.rem(query_id, prot_dev)
        for a in range(prot_dev):
            acc[a] += jnp.where(query == a, result, 0.0)

    def step(i, carry):
        @pl.when(jnp.logical_and(i >= capacity, i < slots))
        def _():
            z_copy(1, i).wait_recv()

            @pl.when(i + window < slots)
            def _():
                z_copy(slot_key(i + window)[0], i + window).start()

            s_copy(i, own_rows).start()

        def tail(k):
            def remote_add(e, inner):
                x_copy(pair_count - 1 - e, k).wait_recv()
                add(r_in[e, k].astype(jnp.float32), pair_tables[e, 0, k])
                return inner

            lax.fori_loop(0, pair_count - 1, remote_add, 0)

        @pl.when(jnp.logical_and(i >= lag, i < slots + lag))
        def _():
            k = i - lag

            @pl.when(k >= capacity)
            def _():
                s_copy(k, sibling_rows).wait_recv()

            weight = weights(k)
            for d in range(1, pair_count):
                there = pair_count - d - 1
                peer = lax.rem(mine + d, pair_count)
                r_out[there, k] = aligned(weight, k, peer).astype(jnp.bfloat16)
                x_copy(d, k).start()
            add(aligned(weight, k, mine), table[0, k])

        @pl.when(i >= lag + 1)
        def _():
            tail(i - lag - 1)

        return carry

    lax.fori_loop(0, slots + lag + 1, step, 0)

    def count(n, counts, ids):
        query = lax.rem(ids(n), prot_dev)
        return tuple(c + jnp.where(query == a, 1, 0) for a, c in enumerate(counts))

    counts = lax.fori_loop(
        0,
        slots,
        lambda n, state: count(n, state, lambda m: table[0, m]),
        (jnp.int32(0),) * prot_dev,
    )
    for e in range(pair_count - 1):
        counts = lax.fori_loop(
            0, slots, lambda n, state: count(n, state, lambda m: pair_tables[e, 0, m]), counts
        )
    for a in range(prot_dev):
        divisor = jnp.full((1, features), jnp.maximum(counts[a], 1).astype(jnp.float32))
        inverse = 1.0 / divisor
        out_buf[a] = (acc[a] * inverse).astype(out_buf.dtype)
        out_copy(a).start()

    for d in range(1, seq_count):
        seq_info_copy(d).wait_send()
    for d in range(1, pair_count):
        pair_info_copy(d).wait_send()
    query_copy().wait_send()

    def finish(i, carry):
        @pl.when(i >= capacity)
        def _():
            z_copy(1, i).wait_send()
            s_copy(i, own_rows).wait_send()

        for d in range(1, pair_count):
            x_copy(d, i).wait_send()
        return carry

    lax.fori_loop(0, slots, finish, 0)
    for a in range(prot_dev):
        out_copy(a).wait()


def local(seq_count, pair_count, embeddings, pairs, lengths):
    prot_dev, half, width = embeddings.shape
    pair_dev = pairs.shape[0]
    full = 2 * half
    features = width // pair_count
    capacity = pair_dev // seq_count
    moved = pair_dev - capacity
    others = pair_count - 1
    smem = pl.BlockSpec(memory_space=pltpu.SMEM)
    dma = pltpu.SemaphoreType.DMA
    bf16 = jnp.bfloat16
    return pl.pallas_call(
        functools.partial(kernel, seq_count, pair_count),
        out_shape=jax.ShapeDtypeStruct((prot_dev, half, features), bf16),
        in_specs=[smem, smem, pl.BlockSpec(memory_space=pl.ANY)],
        out_specs=pl.BlockSpec(memory_space=pl.ANY),
        scratch_shapes=[
            pltpu.SMEM((2, pair_dev), jnp.int32),
            pltpu.SMEM((seq_count - 1, 2, pair_dev), jnp.int32),
            pltpu.SMEM((others, 2, pair_dev), jnp.int32),
            pltpu.VMEM((prot_dev, half, width), bf16),
            pltpu.VMEM((prot_dev, half, width), bf16),
            pltpu.VMEM((moved, half, width), bf16),
            pltpu.VMEM((pair_dev, full, width), bf16),
            pltpu.VMEM((others, pair_dev, half, features), bf16),
            pltpu.VMEM((others, pair_dev, half, features), bf16),
            pltpu.VMEM((prot_dev, half, features), jnp.float32),
            pltpu.VMEM((prot_dev, half, features), bf16),
            dma((prot_dev,)),
            dma,
            dma((seq_count - 1,)),
            dma((seq_count - 1,)),
            dma((others,)),
            dma((others,)),
            dma,
            dma,
            dma((moved,)),
            dma((moved,)),
            dma((moved,)),
            dma((moved,)),
            dma((others, pair_dev)),
            dma((others, pair_dev)),
        ],
        compiler_params=pltpu.CompilerParams(
            collective_id=0, has_side_effects=True, vmem_limit_bytes=60 * 1024 * 1024
        ),
    )(pairs.T, lengths, embeddings)


def solution(mesh):
    placed = (P(("groups", "seq"), "sub", None), P(("groups", "seq", "pair"), None), P("groups"))
    return jax.shard_map(
        functools.partial(local, mesh.shape["seq"], mesh.shape["pair"]),
        mesh=mesh,
        in_specs=placed,
        out_specs=P(("groups", "seq"), "sub", "pair"),
        check_vma=False,
    )
```

```python
import functools
import math

import jax
import jax.numpy as jnp
from jax import lax
from jax.experimental import pallas as pl
from jax.experimental.pallas import tpu as pltpu
from jax.sharding import PartitionSpec as P

masked_fill = -1e30
window = 3
lag = 0
shift = 0
MESH = pl.DeviceIdType.MESH


def kernel(
    seq_count,
    pair_count,
    pairs_ref,
    lengths_ref,
    emb_hbm,
    out_hbm,
    table,
    seq_tables,
    pair_tables,
    emb_ref,
    emb_other,
    outgoing,
    t_own,
    r_out,
    r_in,
    acc,
    out_buf,
    out_sem,
    load_sem,
    seq_info_send,
    seq_info_recv,
    pair_info_send,
    pair_info_recv,
    query_send,
    query_recv,
    z_send,
    z_recv,
    s_send,
    s_recv,
    x_send,
    x_recv,
):
    me = lax.axis_index("seq")
    mine = lax.axis_index("pair")
    sub = lax.axis_index("sub")
    sibling = 1 - sub
    prot_dev, half, width = emb_ref.shape
    full = 2 * half
    pair_dev = pairs_ref.shape[1]
    capacity = pair_dev // seq_count
    slots = pair_dev
    features = width // pair_count
    own_rows = pl.ds(pl.multiple_of(sub * half, half), half)
    sibling_rows = pl.ds(pl.multiple_of(sibling * half, half), half)

    def slot_key(i):
        j = i - capacity
        later = i >= capacity
        d = jnp.where(later, lax.rem(j + shift, seq_count - 1) + 1, 0)
        rank = jnp.where(later, lax.div(j, seq_count - 1), i)
        return d, rank

    def partner(d):
        result = jnp.int32(0)
        bit = 1
        while bit < seq_count:
            result += lax.rem(lax.div(me, bit) + lax.div(jnp.int32(d), bit), 2) * bit
            bit *= 2
        return result

    def seq_peer(d):
        return {"seq": partner(d)}

    def pair_peer(distance):
        return {"pair": lax.rem(mine + distance, pair_count)}

    def feature_block(index):
        return pl.ds(pl.multiple_of(index * features, features), features)

    def remote(src, dst, send, recv, device):
        return pltpu.make_async_remote_copy(
            src_ref=src, dst_ref=dst, send_sem=send, recv_sem=recv, device_id=device,
            device_id_type=MESH,
        )

    def seq_info_copy(d):
        return remote(
            table, seq_tables.at[d - 1], seq_info_send.at[d - 1], seq_info_recv.at[d - 1],
            seq_peer(d),
        )

    def pair_info_copy(d):
        there = pair_count - d - 1
        return remote(
            table, pair_tables.at[there], pair_info_send.at[there], pair_info_recv.at[there],
            pair_peer(d),
        )

    def query_copy():
        return remote(emb_ref, emb_other, query_send, query_recv, {"sub": sibling})

    def z_copy(d, i):
        return remote(
            outgoing.at[i - capacity], t_own.at[i, own_rows, :], z_send.at[i - capacity],
            z_recv.at[i - capacity], seq_peer(d),
        )

    def s_copy(i, rows):
        return remote(
            t_own.at[i, rows, :], t_own.at[i, rows, :], s_send.at[i - capacity],
            s_recv.at[i - capacity], {"sub": sibling},
        )

    def x_copy(d, i):
        there = pair_count - d - 1
        return remote(
            r_out.at[there, i], r_in.at[there, i], x_send.at[there, i], x_recv.at[there, i],
            pair_peer(d),
        )

    def out_copy(a):
        return pltpu.make_async_copy(out_buf.at[a], out_hbm.at[a], out_sem.at[a])

    load = pltpu.make_async_copy(emb_hbm, emb_ref, load_sem)
    load.start()
    barrier = pltpu.get_barrier_semaphore()
    for d in range(1, seq_count):
        pl.semaphore_signal(barrier, inc=1, device_id=seq_peer(d), device_id_type=MESH)
    for d in range(1, pair_count):
        pl.semaphore_signal(barrier, inc=1, device_id=pair_peer(d), device_id_type=MESH)
    pl.semaphore_signal(barrier, inc=1, device_id={"sub": sibling}, device_id_type=MESH)

    def fill_table(i, carry):
        d, rank = slot_key(i)
        owner = partner(d)

        def look(n, state):
            seen, query, target = state
            query_id = pairs_ref[0, n]
            target_id = pairs_ref[1, n]
            match = lax.div(target_id, prot_dev) == owner
            take = jnp.logical_and(match, seen == rank)
            query = jnp.where(take, query_id, query)
            target = jnp.where(take, target_id, target)
            seen = seen + jnp.where(match, 1, 0)
            return (seen, query, target)

        zero = jnp.int32(0)
        _, query, target = lax.fori_loop(
            0, pair_dev, look, (zero, zero, zero), unroll=pair_dev <= 8
        )
        table[0, i] = query
        table[1, i] = target
        return carry

    lax.fori_loop(0, slots, fill_table, 0)
    pl.semaphore_wait(barrier, seq_count + pair_count - 1)

    for d in range(1, seq_count):
        seq_info_copy(d).start()
    for d in range(1, pair_count):
        pair_info_copy(d).start()
    load.wait()
    for d in range(1, seq_count):
        seq_info_copy(d).wait_recv()

    def send_targets(i, carry):
        d, _ = slot_key(i)
        outgoing[i - capacity] = emb_ref[lax.rem(seq_tables[d - 1, 1, i], prot_dev)]

        @pl.when(i < capacity + window)
        def _():
            z_copy(d, i).start()

        return carry

    lax.fori_loop(capacity, slots, send_targets, 0)
    query_copy().start()
    for d in range(1, pair_count):
        pair_info_copy(d).wait_recv()

    def own_targets(i, carry):
        t_own[i, own_rows, :] = emb_ref[lax.rem(table[1, i], prot_dev)]
        return carry

    lax.fori_loop(0, capacity, own_targets, 0)
    acc[...] = jnp.zeros_like(acc)
    query_copy().wait_recv()

    def sibling_targets(i, carry):
        t_own[i, sibling_rows, :] = emb_other[lax.rem(table[1, i], prot_dev)]
        return carry

    lax.fori_loop(0, capacity, sibling_targets, 0)

    scale = 1.0 / math.sqrt(width)
    contract = (((1,), (1,)), ((), ()))

    def weights(i):
        query_id = table[0, i]
        query = lax.rem(query_id, prot_dev)
        query_length = lengths_ref[query_id]
        target_length = lengths_ref[table[1, i]]
        block = t_own[i]
        own = scale * lax.dot_general(
            emb_ref[query], block, contract, preferred_element_type=jnp.float32
        )
        other = scale * lax.dot_general(
            emb_other[query], block, contract, preferred_element_type=jnp.float32
        )
        rows = lax.broadcasted_iota(jnp.int32, (half, full), 0)
        columns = lax.broadcasted_iota(jnp.int32, (half, full), 1)
        own_live = rows + sub * half < query_length
        other_live = rows + sibling * half < query_length
        col_live = columns < target_length
        col_top = jnp.maximum(
            jnp.max(jnp.where(own_live, own, masked_fill), axis=0, keepdims=True),
            jnp.max(jnp.where(other_live, other, masked_fill), axis=0, keepdims=True),
        )
        own_exp = jnp.where(own_live, jnp.exp(own - col_top), 0.0)
        other_exp = jnp.where(other_live, jnp.exp(other - col_top), 0.0)
        col_total = jnp.sum(own_exp, axis=0, keepdims=True) + jnp.sum(
            other_exp, axis=0, keepdims=True
        )
        masked = jnp.where(col_live, own, masked_fill)
        row_exp = jnp.exp(masked - jnp.max(masked, axis=1, keepdims=True))
        row_total = jnp.sum(row_exp, axis=1, keepdims=True)
        both = row_exp * (0.5 / row_total) + own_exp * (0.5 / col_total)
        return jnp.where(jnp.logical_and(own_live, col_live), both, 0.0).astype(jnp.bfloat16)

    def aligned(weight, i, index):
        return jnp.dot(
            weight, t_own[i, :, feature_block(index)], preferred_element_type=jnp.float32
        )

    def add(result, query_id):
        query = lax.rem(query_id, prot_dev)
        for a in range(prot_dev):
            acc[a] += jnp.where(query == a, result, 0.0)

    def step(i, carry):
        @pl.when(jnp.logical_and(i >= capacity, i < slots))
        def _():
            z_copy(1, i).wait_recv()
            s_copy(i, own_rows).start()

            @pl.when(i + window < slots)
            def _():
                z_copy(slot_key(i + window)[0], i + window).start()

        def tail(k):
            def remote_add(e, inner):
                x_copy(pair_count - 1 - e, k).wait_recv()
                add(r_in[e, k].astype(jnp.float32), pair_tables[e, 0, k])
                return inner

            lax.fori_loop(0, pair_count - 1, remote_add, 0)

        @pl.when(jnp.logical_and(i >= lag, i < slots + lag))
        def _():
            k = i - lag

            @pl.when(k >= capacity)
            def _():
                s_copy(k, sibling_rows).wait_recv()

            weight = weights(k)
            for d in range(1, pair_count):
                there = pair_count - d - 1
                peer = lax.rem(mine + d, pair_count)
                r_out[there, k] = aligned(weight, k, peer).astype(jnp.bfloat16)
                x_copy(d, k).start()
            add(aligned(weight, k, mine), table[0, k])

        @pl.when(i >= lag + 1)
        def _():
            tail(i - lag - 1)

        return carry

    lax.fori_loop(0, slots + lag + 1, step, 0)

    def count(n, counts, ids):
        query = lax.rem(ids(n), prot_dev)
        return tuple(c + jnp.where(query == a, 1, 0) for a, c in enumerate(counts))

    counts = lax.fori_loop(
        0,
        slots,
        lambda n, state: count(n, state, lambda m: table[0, m]),
        (jnp.int32(0),) * prot_dev,
    )
    for e in range(pair_count - 1):
        counts = lax.fori_loop(
            0, slots, lambda n, state: count(n, state, lambda m: pair_tables[e, 0, m]), counts
        )
    for a in range(prot_dev):
        divisor = jnp.full((1, features), jnp.maximum(counts[a], 1).astype(jnp.float32))
        inverse = 1.0 / divisor
        out_buf[a] = (acc[a] * inverse).astype(out_buf.dtype)
        out_copy(a).start()

    for d in range(1, seq_count):
        seq_info_copy(d).wait_send()
    for d in range(1, pair_count):
        pair_info_copy(d).wait_send()
    query_copy().wait_send()

    def finish(i, carry):
        @pl.when(i >= capacity)
        def _():
            z_copy(1, i).wait_send()
            s_copy(i, own_rows).wait_send()

        for d in range(1, pair_count):
            x_copy(d, i).wait_send()
        return carry

    lax.fori_loop(0, slots, finish, 0)
    for a in range(prot_dev):
        out_copy(a).wait()


def local(seq_count, pair_count, embeddings, pairs, lengths):
    prot_dev, half, width = embeddings.shape
    pair_dev = pairs.shape[0]
    full = 2 * half
    features = width // pair_count
    capacity = pair_dev // seq_count
    moved = pair_dev - capacity
    others = pair_count - 1
    smem = pl.BlockSpec(memory_space=pltpu.SMEM)
    dma = pltpu.SemaphoreType.DMA
    bf16 = jnp.bfloat16
    return pl.pallas_call(
        functools.partial(kernel, seq_count, pair_count),
        out_shape=jax.ShapeDtypeStruct((prot_dev, half, features), bf16),
        in_specs=[smem, smem, pl.BlockSpec(memory_space=pl.ANY)],
        out_specs=pl.BlockSpec(memory_space=pl.ANY),
        scratch_shapes=[
            pltpu.SMEM((2, pair_dev), jnp.int32),
            pltpu.SMEM((seq_count - 1, 2, pair_dev), jnp.int32),
            pltpu.SMEM((others, 2, pair_dev), jnp.int32),
            pltpu.VMEM((prot_dev, half, width), bf16),
            pltpu.VMEM((prot_dev, half, width), bf16),
            pltpu.VMEM((moved, half, width), bf16),
            pltpu.VMEM((pair_dev, full, width), bf16),
            pltpu.VMEM((others, pair_dev, half, features), bf16),
            pltpu.VMEM((others, pair_dev, half, features), bf16),
            pltpu.VMEM((prot_dev, half, features), jnp.float32),
            pltpu.VMEM((prot_dev, half, features), bf16),
            dma((prot_dev,)),
            dma,
            dma((seq_count - 1,)),
            dma((seq_count - 1,)),
            dma((others,)),
            dma((others,)),
            dma,
            dma,
            dma((moved,)),
            dma((moved,)),
            dma((moved,)),
            dma((moved,)),
            dma((others, pair_dev)),
            dma((others, pair_dev)),
        ],
        compiler_params=pltpu.CompilerParams(
            collective_id=0, has_side_effects=True, vmem_limit_bytes=60 * 1024 * 1024
        ),
    )(pairs.T, lengths, embeddings)


def solution(mesh):
    placed = (P(("groups", "seq"), "sub", None), P(("groups", "seq", "pair"), None), P("groups"))
    return jax.shard_map(
        functools.partial(local, mesh.shape["seq"], mesh.shape["pair"]),
        mesh=mesh,
        in_specs=placed,
        out_specs=P(("groups", "seq"), "sub", "pair"),
        check_vma=False,
    )
```
